512 devices in a mesh: wide: 32 (over x, y, core), narrow: 16 (over z).
Axes of the slice: x: 4, y: 4, z: 16, core: 2. Of those that a mesh axis runs over, the one named last changes fastest.
Arguments:
- activations: bfloat16 [65536, 4096], P(('wide', 'narrow')), may hold values from -24 to 24
- grad_gate: bfloat16 [65536, 7168], P(('wide', 'narrow')), may hold values from -24 to 24
- grad_up: bfloat16 [65536, 7168], P(('wide', 'narrow')), may hold values from -24 to 24
- state_gate: float32 [7168, 64], P(('wide', 'narrow')), may hold values from -6 to 6
- state_up: float32 [7168, 64], P(('wide', 'narrow')), may hold values from -6 to 6
Outputs:
- left_gate: float32 [4096, 64], P(('wide', 'narrow'))
- right_gate: float32 [7168, 64], P(('wide', 'narrow'))
- left_up: float32 [4096, 64], P(('wide', 'narrow'))
- right_up: float32 [7168, 64], P(('wide', 'narrow'))
The draws below stay inside these ranges and needn't reach their ends.
All inputs are finite; a program needn't handle non-finite values.
Results may differ from the reference program's by a relative error of at most 0.0004.
Values sent between devices are 32-bit elements; how exact they have to be, the bound alone decides.
No kernel may reach another device: no remote copies, remote signals or barrier semaphores. Data moves between devices by JAX's collectives and lax.ppermute only.
A program may use at most 64 MiB of HBM per device.

```python
import math
import jax
import jax.numpy as jnp
from jax import lax

D = 4096
FW = 7168
RANK = 64
TOK_DEV = 128
TOKENS = 65536


def draw_activations(key, part):
    key = jax.random.fold_in(key, 11)
    key_base, key_cols = jax.random.split(key, 2)
    columns = 0.3 * jnp.exp(jax.random.uniform(key_cols, (D,), jnp.float32, 0.0, math.log(10.0)))
    position = jnp.arange(TOKENS, dtype=jnp.float32) / jnp.float32(TOKENS)
    base = jax.random.normal(key_base, (TOKENS, D), jnp.float32)
    rise = jnp.exp(math.log(3.0) * position)
    values = jnp.clip(base, -4.0, 4.0) * columns[None, :] * (0.6 * rise)[:, None]
    return jnp.clip(values, -24.0, 24.0).astype(jnp.bfloat16)


def raised(values, own_key, source, target, parts, factor):
    def block_of(dim):
        return (jnp.arange(values.shape[dim]) // (values.shape[dim] // parts)).reshape((-1,) + (1,) * (values.ndim - 1 - dim))

    one_side = jax.random.permutation(own_key, parts)[block_of(target)]
    second = (block_of(target) + parts // 2) % parts
    return jnp.where((block_of(source) == one_side) | (block_of(source) == second), factor * values, values)


def level_of(stream_key, shape, shards, smallest, top_value):
    def one(dim, shards_of):
        draws = jax.random.uniform(jax.random.fold_in(jax.random.fold_in(stream_key, 6), dim), (shards_of,), jnp.float32, smallest / len(shards), top_value / len(shards))
        return jnp.repeat(jnp.exp(draws), shape[dim] // shards_of).reshape((-1,) + (1,) * (len(shape) - dim - 1))

    factor_of = one(*shards[0])
    for cut in shards[1:]:
        factor_of = factor_of * one(*cut)
    return factor_of


def gaussian(rng, dims, width, reach, cuts=(), kind=jnp.bfloat16):
    entries = width * jax.random.normal(rng, dims, jnp.float32)
    if cuts:
        entries = entries * level_of(rng, dims, cuts, -0.22, 0.18)
    return jnp.clip(entries, -reach, reach).astype(kind)


def gaussian_with(stream_key, shape, width, most, pieces, heavy, kind=jnp.bfloat16):
    result = width * jax.random.normal(stream_key, shape, jnp.float32)
    if pieces:
        result = result * level_of(stream_key, shape, pieces, -0.22, 0.18)
    return jnp.clip(raised(result, jax.random.fold_in(stream_key, 3), *heavy), -most, most).astype(kind)


def setup_inputs(seed: int = 0) -> dict:
    seeds = jax.random.split(jax.random.key(seed), 6)
    return {
        "activations": draw_activations(jax.random.fold_in(seeds[5], 71), 0),
        "grad_gate": gaussian_with(seeds[1], (TOKENS, FW), 1.0, 24.0, ((0, 512),), (0, 1, 512, 6.0)),
        "grad_up": gaussian_with(seeds[2], (TOKENS, FW), 1.0, 24.0, ((0, 512),), (0, 1, 512, 6.0)),
        "state_gate": gaussian(seeds[3], (FW, RANK), 1.0, 6.0, ((0, 512),), jnp.float32),
        "state_up": gaussian(seeds[4], (FW, RANK), 1.0, 6.0, ((0, 512),), jnp.float32),
    }


HIGH = lax.Precision.HIGHEST

def left_sum(activations, grads, state):
    blocks = TOKENS // TOK_DEV
    act_blocks = activations.reshape(blocks, TOK_DEV, D)
    grad_blocks = grads.reshape(blocks, TOK_DEV, FW)

    def step(total, pair):
        act, grad = pair
        small = jnp.dot(grad.astype(jnp.float32), state.astype(jnp.float32), precision=HIGH, preferred_element_type=jnp.float32)
        return (total + jnp.dot(act.astype(jnp.float32).T.astype(jnp.float32), small.astype(jnp.float32), precision=HIGH, preferred_element_type=jnp.float32), None)
    total, _ = lax.scan(step, jnp.zeros((D, RANK), jnp.float32), (act_blocks, grad_blocks))
    return total / jnp.float32(math.sqrt(TOKENS))

def right_sum(activations, grads, basis):
    blocks = TOKENS // TOK_DEV
    act_blocks = activations.reshape(blocks, TOK_DEV, D)
    grad_blocks = grads.reshape(blocks, TOK_DEV, FW)

    def step(total, pair):
        act, grad = pair
        small = jnp.dot(act.astype(jnp.float32), basis.astype(jnp.float32), precision=HIGH, preferred_element_type=jnp.float32)
        return (total + jnp.dot(grad.astype(jnp.float32).T.astype(jnp.float32), small.astype(jnp.float32), precision=HIGH, preferred_element_type=jnp.float32), None)
    total, _ = lax.scan(step, jnp.zeros((FW, RANK), jnp.float32), (act_blocks, grad_blocks))
    return total / jnp.float32(math.sqrt(TOKENS))

def compress(activations, grads, state):
    raw = left_sum(activations, grads, state)
    gram = jnp.dot(raw.T.astype(jnp.float32), raw.astype(jnp.float32), precision=HIGH, preferred_element_type=jnp.float32)
    lower = jnp.linalg.cholesky(gram)
    basis = lax.linalg.triangular_solve(lower, raw, left_side=False, lower=True, transpose_a=True)
    right = right_sum(activations, grads, basis)
    return (basis * jnp.float32(math.sqrt(D)), right)

def reference(activations, grad_gate, grad_up, state_gate, state_up):
    left_gate, right_gate = compress(activations, grad_gate, state_gate)
    left_up, right_up = compress(activations, grad_up, state_up)
    return (left_gate, right_gate, left_up, right_up)
```

```python
import math

import jax
import jax.numpy as jnp
from jax import lax
from jax.sharding import Mesh, PartitionSpec as P

HIGH = lax.Precision.HIGHEST
PLANE = ("x", "y")
EVERY = ("x", "y", "core", "z")


def parts_of(value):
    first = lax.reduce_precision(value, 8, 7)
    rest = value - first
    second = lax.reduce_precision(rest, 8, 7)
    third = rest - second
    return [piece.astype(jnp.bfloat16) for piece in (first, second, third)]


def exact_dot(left, right, contract):
    columns = right.shape[1]
    joined = jnp.concatenate(parts_of(right), axis=1)
    wide = lax.dot_general(
        left, joined, (((contract,), (0,)), ((), ())), preferred_element_type=jnp.float32
    )
    return wide[:, :columns] + wide[:, columns : 2 * columns] + wide[:, 2 * columns :]


def exchange(value, axes):
    return lax.all_to_all(value, axes, 0, 0, tiled=True)


def spread(block, axes):
    count = lax.axis_size(axes)
    return exchange(jnp.broadcast_to(block[None], (count, *block.shape)), axes)


def other_core(value):
    return lax.ppermute(value, "core", [(0, 1), (1, 0)])


def gather_rows(block):
    rows, columns = block.shape
    line = spread(block, "z").reshape(-1, columns)
    plane = spread(line, PLANE)
    other = other_core(plane)
    first = lax.axis_index("core") == 0
    whole = jnp.stack(
        [jnp.where(first, plane, other), jnp.where(first, other, plane)], axis=1
    )
    return whole.reshape(-1, columns)


def scatter_rows(whole):
    columns = whole.shape[1]
    core = lax.axis_index("core")
    count = lax.axis_size(PLANE)
    lines = whole.reshape(count, 2, -1, columns)
    keep = lax.dynamic_index_in_dim(lines, core, 1, keepdims=False)
    give = lax.dynamic_index_in_dim(lines, 1 - core, 1, keepdims=False)
    chip = keep + other_core(give)
    line = jnp.sum(exchange(chip, PLANE), axis=0)
    stack = line.reshape(lax.axis_size("z"), -1, columns)
    return jnp.sum(exchange(stack, "z"), axis=0)


def shards(activations, grad_gate, grad_up, state_gate, state_up):
    devices = lax.axis_size(EVERY)
    factor = jnp.float32(1.0 / math.sqrt(activations.shape[0] * devices))
    width = activations.shape[1]
    rank = state_gate.shape[1]

    state = gather_rows(jnp.concatenate([state_gate, state_up], axis=1))
    small = jnp.concatenate(
        [exact_dot(grad_gate, state[:, :rank], 1), exact_dot(grad_up, state[:, rank:], 1)],
        axis=1,
    )
    mine = scatter_rows(exact_dot(activations, small, 0)) * factor
    raw = gather_rows(mine)

    project = exact_dot(activations, raw, 1) * factor
    joined = jnp.concatenate(
        [
            exact_dot(grad_gate, project[:, :rank], 0),
            exact_dot(grad_up, project[:, rank:], 0),
        ],
        axis=1,
    )
    summed = scatter_rows(joined)

    gram = lax.dot_general(
        raw, raw, (((0,), (0,)), ((), ())), precision=HIGH, preferred_element_type=jnp.float32
    )
    lower = jnp.linalg.cholesky(
        jnp.stack([gram[:rank, :rank], gram[rank:, rank:]]), symmetrize_input=False
    )
    rows = jnp.concatenate([mine, summed], axis=0)
    rows = jnp.stack([rows[:, :rank], rows[:, rank:]])
    solved = lax.linalg.triangular_solve(
        lower, rows, left_side=False, lower=True, transpose_a=True
    )
    stretch = jnp.float32(math.sqrt(width))
    own = mine.shape[0]
    left = solved[:, :own] * stretch
    right = solved[:, own:]
    return (left[0], right[0], left[1], right[1])


def solution(mesh):
    wide, narrow = mesh.devices.shape
    side = math.isqrt(wide // 2)
    fine = Mesh(mesh.devices.reshape(side, side, 2, narrow), EVERY)
    rows = P(EVERY, None)
    return jax.shard_map(
        shards,
        mesh=fine,
        in_specs=(rows,) * 5,
        out_specs=(rows,) * 4,
        check_vma=False,
    )
```

```python
import functools
import math

import jax
import jax.numpy as jnp
from jax import lax
from jax.experimental import pallas as pl
from jax.experimental.pallas import tpu as pltpu
from jax.sharding import Mesh, PartitionSpec as P

HIGH = lax.Precision.HIGHEST
PLANE = ("x", "y")
EVERY = ("x", "y", "core", "z")
PARAMS = pltpu.CompilerParams(vmem_limit_bytes=20 * 1024 * 1024)


def exchange(value, axes):
    return lax.all_to_all(value, axes, 0, 0, tiled=True)


def spread(block, axes):
    count = lax.axis_size(axes)
    return exchange(jnp.broadcast_to(block[None], (count, *block.shape)), axes)


def other_core(value):
    return lax.ppermute(value, "core", [(0, 1), (1, 0)])


def gather_line(block):
    return spread(block, "z").reshape(-1, block.shape[1])


def gather_plane(block):
    return spread(block, PLANE).reshape(-1, block.shape[1])


def scatter_rows(whole):
    columns = whole.shape[1]
    chip = whole.reshape(lax.axis_size(PLANE), -1, columns)
    line = jnp.sum(exchange(chip, PLANE), axis=0)
    stack = line.reshape(lax.axis_size("z"), -1, columns)
    return jnp.sum(exchange(stack, "z"), axis=0)


def in_vmem(kernel, *shapes, first=()):
    single = len(shapes) == 1

    def call(*values):
        places = [*first, *[pltpu.VMEM] * (len(values) - len(first))]
        return pl.pallas_call(
            kernel,
            out_shape=shapes[0] if single else shapes,
            in_specs=[pl.BlockSpec(memory_space=place) for place in places],
            compiler_params=PARAMS,
            cost_estimate=pl.CostEstimate(flops=1, bytes_accessed=1, transcendentals=0),
        )(*values)

    return call


def shape_of(rows, columns, kind=jnp.float32):
    return jax.ShapeDtypeStruct((rows, columns), kind)


def sorted_blocks(core_ref, count, own, value_refs, write):
    def walk(kept):
        place = 0
        for value_ref in value_refs:
            block = value_ref.shape[1] // (2 * count)
            for i in range(count):
                start = (2 * i + kept) * block
                write(value_ref[:, start : start + block], place, place + block)
                place += block

    pl.when(core_ref[0] == (0 if own else 1))(lambda: walk(0))
    pl.when(core_ref[0] == (1 if own else 0))(lambda: walk(1))


def give_kernel(count, core_ref, after_ref, *refs):
    del after_ref
    inputs = 3
    ends = []
    for ref in refs[inputs:]:
        ends.append(ref.shape[1] + (ends[-1] if ends else 0))

    def write(value, start, stop):
        which = next(i for i, end in enumerate(ends) if stop <= end)
        base = ends[which] - refs[inputs + which].shape[1]
        refs[inputs + which][:, start - base : stop - base] = value.astype(jnp.float32)

    sorted_blocks(core_ref, count, False, refs[:inputs], write)


def give(core, after, *values):
    tokens = values[0].shape[0]
    pieces = [1, 2, 2]
    widths = [v.shape[1] // 2 // n for v, n in zip(values, pieces) for _ in range(n)]
    return in_vmem(
        functools.partial(give_kernel, lax.axis_size(PLANE)),
        *[shape_of(tokens, width) for width in widths],
        first=(pltpu.SMEM, pl.ANY),
    )(core.reshape(1), after, *values)


def keep_kernel(count, core_ref, after_ref, *refs):
    del after_ref
    *value_refs, rows_ref, turned_ref = refs

    def write(value, start, stop):
        rows_ref[:, start:stop] = value

    sorted_blocks(core_ref, count, True, value_refs, write)
    turned_ref[...] = rows_ref[...].astype(jnp.float32).T.astype(jnp.bfloat16)


def keep(core, after, *values):
    tokens = values[0].shape[0]
    columns = sum(v.shape[1] for v in values) // 2
    return in_vmem(
        functools.partial(keep_kernel, lax.axis_size(PLANE)),
        shape_of(tokens, columns, jnp.bfloat16),
        shape_of(columns, tokens, jnp.bfloat16),
        first=(pltpu.SMEM, pl.ANY),
    )(core.reshape(1), after, *values)


def merge_kernel(groups, kept_ref, turned_ref, *refs):
    tokens = kept_ref.shape[0]
    pieces, outs = refs[: sum(groups)], refs[sum(groups) :]
    place = 0
    for rows_out, turned_out, count in zip(outs[::2], outs[1::2], groups):
        width = rows_out.shape[1]
        rows_out[:tokens, :] = kept_ref[:, place : place + width]
        turned_out[:, :tokens] = turned_ref[place : place + width, :]
        place += width
        start = 0
        for piece_ref in pieces[:count]:
            to = slice(start, start + piece_ref.shape[1])
            piece = piece_ref[...]
            rows_out[tokens:, to] = piece.astype(jnp.bfloat16)
            turned_out[to, tokens:] = piece.T.astype(jnp.bfloat16)
            start = to.stop
        pieces = pieces[count:]


def merge(kept, turned, pieces, groups):
    tokens = 2 * kept.shape[0]
    shapes, rest = [], list(pieces)
    for count in groups:
        width = sum(p.shape[1] for p in rest[:count])
        rest = rest[count:]
        shapes += [shape_of(tokens, width, jnp.bfloat16), shape_of(width, tokens, jnp.bfloat16)]
    return in_vmem(functools.partial(merge_kernel, groups), *shapes)(kept, turned, *pieces)


def halves(value):
    high = value.astype(jnp.bfloat16)
    low = (value - high.astype(jnp.float32)).astype(jnp.bfloat16)
    return jnp.concatenate([high, low], axis=1)


def fold(value):
    columns = value.shape[1] // 2
    return value[:, :columns] + value[:, columns:]


def product(left, right):
    return fold(jnp.dot(left, right, preferred_element_type=jnp.float32))


def joined(gate, up):
    lane = lax.broadcasted_iota(jnp.int32, gate.shape, 1)
    return jnp.where(lane < gate.shape[1] // 2, gate, up)


def swapped(mine, other):
    tokens = mine.shape[0] // 2
    return jnp.concatenate(
        [mine[:tokens] + other[tokens:], mine[tokens:] + other[:tokens]], axis=0
    )


def small_kernel(rows_ref, state_ref, out_ref):
    state = halves(state_ref[...])
    columns = state.shape[0]
    out_ref[...] = joined(
        product(rows_ref[:, :columns], state),
        product(rows_ref[:, columns:], state),
    )


def raw_kernel(turned_ref, mine_ref, other_ref, out_ref):
    small = halves(swapped(mine_ref[...], other_ref[...]))
    out_ref[...] = product(turned_ref[...], small)


def project_kernel(factor, rows_ref, raw_ref, out_ref):
    out_ref[...] = product(rows_ref[...], halves(raw_ref[...])) * factor


def right_kernel(turned_ref, mine_ref, other_ref, out_ref):
    project = halves(swapped(mine_ref[...], other_ref[...]))
    columns = out_ref.shape[0]
    out_ref[...] = joined(
        product(turned_ref[:columns, :], project),
        product(turned_ref[columns:, :], project),
    )


def shards(activations, grad_gate, grad_up, state_gate, state_up):
    devices = lax.axis_size(EVERY)
    core = lax.axis_index("core")
    tokens, width = activations.shape
    factor = 1.0 / math.sqrt(tokens * devices)
    rank = state_gate.shape[1]
    both = 2 * rank

    line = gather_line(jnp.concatenate([state_gate, state_up], axis=1))
    values = (activations, grad_gate, grad_up)
    taken = [other_core(piece) for piece in give(core, line, *values)]
    kept, turned = keep(core, line, *values)
    state = gather_plane(line)
    act, act_turned, grad, grad_turned = merge(kept, turned, taken, (1, 4))

    small = in_vmem(small_kernel, shape_of(2 * tokens, both))(grad, state)
    partial = in_vmem(raw_kernel, shape_of(width // 2, both))(
        act_turned, small, other_core(small)
    )
    mine = scatter_rows(partial) * jnp.float32(factor)
    raw = gather_plane(gather_line(mine))

    project = in_vmem(
        functools.partial(project_kernel, factor), shape_of(2 * tokens, both)
    )(act, raw)
    partial = in_vmem(right_kernel, shape_of(state.shape[0], both))(
        grad_turned, project, other_core(project)
    )
    summed = scatter_rows(partial)

    gram = lax.dot_general(
        raw, raw, (((0,), (0,)), ((), ())), precision=HIGH, preferred_element_type=jnp.float32
    )
    gram = gram + other_core(gram)
    lower = jnp.linalg.cholesky(
        jnp.stack([gram[:rank, :rank], gram[rank:, rank:]]), symmetrize_input=False
    )
    rows = jnp.concatenate([mine, summed], axis=0)
    rows = jnp.stack([rows[:, :rank], rows[:, rank:]])
    solved = lax.linalg.triangular_solve(
        lower, rows, left_side=False, lower=True, transpose_a=True
    )
    stretch = jnp.float32(math.sqrt(width))
    own = mine.shape[0]
    left = solved[:, :own] * stretch
    right = solved[:, own:]
    return (left[0], right[0], left[1], right[1])


def solution(mesh):
    wide, narrow = mesh.devices.shape
    side = math.isqrt(wide // 2)
    fine = Mesh(mesh.devices.reshape(side, side, 2, narrow), EVERY)
    rows = P(EVERY, None)
    return jax.shard_map(
        shards,
        mesh=fine,
        in_specs=(rows,) * 5,
        out_specs=(rows,) * 4,
        check_vma=False,
    )
```

```python
import functools
import math

import jax
import jax.numpy as jnp
from jax import lax
from jax.experimental import pallas as pl
from jax.experimental.pallas import tpu as pltpu
from jax.sharding import Mesh, PartitionSpec as P

HIGH = lax.Precision.HIGHEST
PLANE = ("x", "y")
LINE = ("core", "z")
EVERY = ("x", "y", "core", "z")
PARAMS = pltpu.CompilerParams(vmem_limit_bytes=40 * 1024 * 1024)
LIGHT = pl.CostEstimate(flops=1, bytes_accessed=1, transcendentals=0)


def exchange(value, axes):
    return lax.all_to_all(value, axes, 0, 0, tiled=True)


def spread(block, axes):
    count = lax.axis_size(axes)
    return exchange(jnp.broadcast_to(block[None], (count, *block.shape)), axes)


def other_core(value):
    return lax.ppermute(value, "core", [(0, 1), (1, 0)])


def gather_plane(block):
    return spread(block, PLANE).reshape(-1, block.shape[1])


def scatter_plane(whole):
    chip = whole.reshape(lax.axis_size(PLANE), -1, whole.shape[1])
    return jnp.sum(exchange(chip, PLANE), axis=0)


def to_core(pair):
    return exchange(pair.reshape(-1, *pair.shape[2:]), LINE).reshape(pair.shape)


def in_hbm(*values):
    return [pltpu.with_memory_space_constraint(v, pltpu.HBM) for v in values]


def call(kernel, shapes, memories, scratch=(), light=False, written=False, **options):
    return pl.pallas_call(
        kernel,
        out_shape=shapes,
        in_specs=[pl.BlockSpec(memory_space=m) for m in memories],
        out_specs=jax.tree.map(
            lambda s: pl.BlockSpec(
                memory_space=pl.ANY if s.memory_space == pltpu.HBM and not written else pltpu.VMEM
            ),
            shapes,
        ),
        scratch_shapes=list(scratch),
        compiler_params=PARAMS,
        cost_estimate=LIGHT if light else None,
        **options,
    )


def sorted_blocks(count, value_ref):
    block = value_ref.shape[1] // (2 * count)
    for half in range(2):
        for i in range(count):
            start = (2 * i + half) * block
            place = (half * count + i) * block
            yield value_ref[:, start : start + block], slice(place, place + block)


def write_halves(count, value_ref, low_out, high_out):
    half = low_out.shape[1]
    for value, to in sorted_blocks(count, value_ref):
        if to.stop <= half:
            low_out[:, to] = value.astype(jnp.float32)
        else:
            high_out[:, to.start - half : to.stop - half] = value.astype(jnp.float32)


def give_grad_kernel(count, gate_ref, up_ref, low_out, high_out, buffer, sem):
    core = lax.axis_index("core")
    for which, ref in ((0, up_ref), (1, gate_ref)):

        @pl.when(core == which)
        def _(ref=ref):
            copy = pltpu.make_async_copy(ref, buffer, sem)
            copy.start()
            copy.wait()

    write_halves(count, buffer, low_out, high_out)


def give_act_kernel(count, act_ref, low_out, high_out):
    write_halves(count, act_ref, low_out, high_out)


def give(act, gate, up):
    count = lax.axis_size(PLANE)
    tokens, columns = gate.shape
    grads = [pltpu.VMEM((tokens, columns // 2), jnp.float32)] * 2
    grads = call(
        functools.partial(give_grad_kernel, count),
        grads,
        [pl.ANY] * 2,
        [pltpu.VMEM((tokens, columns), gate.dtype), pltpu.SemaphoreType.DMA],
        light=True,
    )(*in_hbm(gate, up))
    acts = [pltpu.VMEM((tokens, act.shape[1] // 2), jnp.float32)] * 2
    acts = call(functools.partial(give_act_kernel, count), acts, [pltpu.VMEM], light=True)(act)
    return *acts, *grads


def turn(value):
    return value.astype(jnp.float32).T.astype(jnp.bfloat16)


def own_stores(outs, scratch):
    tokens = scratch[0].shape[0]
    staged, sems = scratch[2:6], scratch[6]
    return [
        pltpu.make_async_copy(
            staged[i],
            outs[i].at[:, :tokens] if i % 2 else outs[i].at[:tokens, :],
            sems.at[2 + i],
        )
        for i in range(4)
    ]


def own_part(count, act_ref, grad_ref, outs, scratch):
    staged, sems = scratch[2:6], scratch[6]
    loads = [
        pltpu.make_async_copy(ref, scratch[i], sems.at[i])
        for i, ref in enumerate((act_ref, grad_ref))
    ]
    for load in loads:
        load.start()
    stores = own_stores(outs, scratch)
    for i in range(2):
        rows, turned = staged[2 * i : 2 * i + 2]
        loads[i].wait()
        for value, to in sorted_blocks(count, scratch[i]):
            rows[:, to] = value
        stores[2 * i].start()
        turned[...] = turn(rows[...])
        stores[2 * i + 1].start()


def keep_kernel(count, line_ref, act_ref, gate_ref, lines_out, *refs):
    outs, scratch, line_sem = refs[:4], refs[4:-1], refs[-1]
    copies = [
        pltpu.make_async_copy(line_ref, lines_out.at[i], line_sem.at[i]) for i in range(count)
    ]
    for copy in copies:
        copy.start()

    @pl.when(lax.axis_index("core") == 0)
    def _():
        own_part(count, act_ref, gate_ref, outs, scratch)
        for store in own_stores(outs, scratch):
            store.wait()

    for copy in copies:
        copy.wait()


def merge_kernel(count, act_ref, up_ref, *refs):
    takes, outs, scratch, others = refs[:4], refs[8:12], refs[12:19], refs[19:]
    buffers, staged, (load_sems, store_sems) = others[:4], others[4:8], others[8:]
    loads = [
        pltpu.make_async_copy(take, buffer, load_sems.at[i])
        for i, (take, buffer) in enumerate(zip(takes, buffers))
    ]
    for load in loads:
        load.start()

    @pl.when(lax.axis_index("core") == 1)
    def _():
        own_part(count, act_ref, up_ref, outs, scratch)

    tokens = buffers[0].shape[0]
    stores = []
    for i in range(2):
        rows, turned = staged[2 * i : 2 * i + 2]
        half = buffers[2 * i].shape[1]
        for j in range(2):
            loads[2 * i + j].wait()
            to = slice(j * half, (j + 1) * half)
            value = buffers[2 * i + j][...]
            rows[:, to] = value.astype(jnp.bfloat16)
            turned[to, :] = value.T.astype(jnp.bfloat16)
        stores += [
            pltpu.make_async_copy(rows, outs[2 * i].at[tokens:, :], store_sems.at[2 * i]),
            pltpu.make_async_copy(
                turned, outs[2 * i + 1].at[:, tokens:], store_sems.at[2 * i + 1]
            ),
        ]
        for store in stores[-2:]:
            store.start()
    for store in stores:
        store.wait()

    @pl.when(lax.axis_index("core") == 1)
    def _():
        for store in own_stores(outs, scratch):
            store.wait()


def chip_arrays(act, gate, up, line, taken):
    count = lax.axis_size(PLANE)
    tokens = act.shape[0]
    kinds = [
        (shape, act.dtype)
        for v in (act, gate)
        for shape in ((tokens, v.shape[1]), (v.shape[1], tokens))
    ]
    scratch = [
        pltpu.VMEM(act.shape, act.dtype),
        pltpu.VMEM(gate.shape, gate.dtype),
        *[pltpu.VMEM(*kind) for kind in kinds],
        pltpu.SemaphoreType.DMA((6,)),
    ]
    wholes = [
        pltpu.HBM(tuple(2 * n if n == tokens else n for n in shape), kind)
        for shape, kind in kinds
    ]
    lines, *partly = call(
        functools.partial(keep_kernel, count),
        [pltpu.HBM((count, *line.shape), line.dtype), *wholes],
        [pltpu.VMEM, pl.ANY, pl.ANY],
        [*scratch, pltpu.SemaphoreType.DMA((count,))],
        light=True,
    )(line, *in_hbm(act, gate))

    def finish():
        buffers = [pltpu.VMEM(t.shape, t.dtype) for t in taken]
        sems = [pltpu.SemaphoreType.DMA((4,))] * 2
        return call(
            functools.partial(merge_kernel, count),
            wholes,
            [pl.ANY] * 10,
            [*scratch, *buffers, *scratch[2:6], *sems],
            light=True,
            input_output_aliases={6 + i: i for i in range(4)},
        )(*in_hbm(act, up, *taken), *partly)

    return lines, finish


def halves(value):
    high = value.astype(jnp.bfloat16)
    low = (value - high.astype(jnp.float32)).astype(jnp.bfloat16)
    return jnp.concatenate([high, low], axis=1)


def fold(value):
    columns = value.shape[1] // 2
    return value[:, :columns] + value[:, columns:]


def product(left, right):
    return fold(jnp.dot(left, right, preferred_element_type=jnp.float32))


def joined(low, high):
    lane = lax.broadcasted_iota(jnp.int32, low.shape, 1)
    return jnp.where(lane < low.shape[1] // 2, low, high)


def doubled(value):
    return value + pltpu.roll(value, value.shape[1] // 2, 1)


def small_kernel(grad_ref, state_ref, out_ref, buffer, sems):
    steps = sems.shape[0]
    step = grad_ref.shape[0] // steps
    copies = []
    for i in range(steps):
        at = slice(i * step, (i + 1) * step)
        copies.append(pltpu.make_async_copy(grad_ref.at[at, :], buffer.at[at, :], sems.at[i]))
        copies[-1].start()
    state = halves(state_ref[...])
    columns = state.shape[0]
    for i in range(steps):
        at = slice(i * step, (i + 1) * step)
        copies[i].wait()
        out_ref[at, :] = doubled(
            joined(product(buffer[at, :columns], state), product(buffer[at, columns:], state))
        )


def tall_kernel(turned_ref, factor_ref, out_ref):
    factor = halves(factor_ref[...])
    rows = out_ref.shape[0]
    out_ref[...] = joined(
        product(turned_ref[:rows, :], factor), product(turned_ref[rows:, :], factor)
    )


def tall_product(turned, factor):
    shape = (turned.shape[0] // 2, factor.shape[1])
    return call(tall_kernel, pltpu.VMEM(shape, jnp.float32), [pltpu.VMEM] * 2)(turned, factor)


def streamed_kernel(turned_ref, factor_ref, out_ref, staged, sems):
    factor = halves(factor_ref[...])
    steps = sems.shape[0]
    rows = out_ref.shape[0]
    step = rows // steps
    copies = []
    for i in range(steps):
        at = slice(i * step, (i + 1) * step)
        other = slice(rows + i * step, rows + (i + 1) * step)
        staged[at, :] = joined(
            product(turned_ref[at, :], factor), product(turned_ref[other, :], factor)
        )
        copies.append(pltpu.make_async_copy(staged.at[at, :], out_ref.at[at, :], sems.at[i]))
        copies[-1].start()
    for copy in copies:
        copy.wait()


def streamed_product(turned, factor):
    shape = (turned.shape[0] // 2, factor.shape[1])
    return call(
        streamed_kernel,
        pltpu.HBM(shape, jnp.float32),
        [pltpu.VMEM] * 2,
        [pltpu.VMEM(shape, jnp.float32), pltpu.SemaphoreType.DMA((4,))],
    )(turned, factor)


def project_kernel(factor, rows_ref, raw_ref, out_ref):
    raw = halves(raw_ref[...])
    columns = raw.shape[0]
    out_ref[...] = factor * doubled(
        joined(product(rows_ref[:, :columns], raw), product(rows_ref[:, columns:], raw))
    )


def pack_kernel(after_ref, inverse_ref, rows_ref, out_ref):
    del after_ref
    rank = inverse_ref.shape[0]
    out_ref[:rank, :rank] = inverse_ref[...]
    out_ref[:rank, rank:] = jnp.zeros_like(inverse_ref)
    out_ref[rank:, :] = rows_ref[...]


def pack(after, inverse, rows):
    shape = (inverse.shape[0] + rows.shape[0], rows.shape[1])
    return call(
        pack_kernel, pltpu.VMEM(shape, jnp.float32), [pl.ANY, pltpu.VMEM, pltpu.VMEM], light=True
    )(after, inverse, rows)


def end_kernel(stretch, parts_ref, mine_ref, other_ref, *outs):
    rank = outs[0].shape[1]
    core = lax.axis_index("core")

    def dot(left, right):
        return jnp.dot(left, right, precision=HIGH, preferred_element_type=jnp.float32)

    def write(own):
        for which, ref in enumerate((mine_ref, other_ref) if own == 0 else (other_ref, mine_ref)):
            inverse = ref[:rank, :rank]
            rows = ref[rank:, own * rank : (own + 1) * rank]
            outs[2 * which][...] = dot(rows, inverse) * stretch
            outs[2 * which + 1][...] = dot(jnp.sum(parts_ref[which], axis=0), inverse)

    pl.when(core == 0)(lambda: write(0))
    pl.when(core == 1)(lambda: write(1))


def shards(activations, grad_gate, grad_up, state_gate, state_up):
    devices = lax.axis_size(EVERY)
    tokens, width = activations.shape
    factor = 1.0 / math.sqrt(tokens * devices)
    rows, rank = state_gate.shape
    both = 2 * rank
    line_size = lax.axis_size("z")

    states = jnp.stack([state_gate, state_up])[:, None]
    states = to_core(jnp.broadcast_to(states, (2, line_size, rows, rank)))
    line = jnp.concatenate([states[0], states[1]], axis=-1).reshape(-1, both)

    taken = [other_core(piece) for piece in give(activations, grad_gate, grad_up)]
    lines, finish = chip_arrays(activations, grad_gate, grad_up, line, taken)
    state = exchange(lines, PLANE).reshape(-1, both)
    act, act_turned, grad, grad_turned = finish()

    small = call(
        small_kernel,
        pltpu.VMEM((2 * tokens, both), jnp.float32),
        [pl.ANY, pltpu.VMEM],
        [pltpu.VMEM(grad.shape, grad.dtype), pltpu.SemaphoreType.DMA((2,))],
    )(*in_hbm(grad), state)
    summed = scatter_plane(tall_product(act_turned, small)).reshape(line_size, -1, both)
    mine = jnp.sum(exchange(summed, "z"), axis=0) * jnp.float32(factor)
    raw = gather_plane(spread(mine, "z").reshape(-1, both))

    project = call(
        functools.partial(project_kernel, factor),
        pltpu.VMEM((2 * tokens, both), jnp.float32),
        [pltpu.VMEM] * 2,
    )(act, raw)
    summed = scatter_plane(streamed_product(grad_turned, project)).reshape(line_size, rows, both)
    parts = to_core(jnp.stack([summed[..., :rank], summed[..., rank:]]))

    gram = lax.dot_general(
        raw, raw, (((0,), (0,)), ((), ())), precision=HIGH, preferred_element_type=jnp.float32
    )
    gram = gram[:rank, :rank] + gram[rank:, rank:]
    lower = jnp.linalg.cholesky(gram, symmetrize_input=False)
    inverse = lax.linalg.triangular_solve(
        lower, jnp.eye(rank, dtype=jnp.float32), left_side=False, lower=True, transpose_a=True
    )
    packed = pack(summed, inverse, mine)

    shapes = [pltpu.HBM((n, rank), jnp.float32) for _ in range(2) for n in (mine.shape[0], rows)]
    return tuple(
        call(
            functools.partial(end_kernel, math.sqrt(width)), shapes, [pltpu.VMEM] * 3, written=True
        )(parts, packed, other_core(packed))
    )


def solution(mesh):
    wide, narrow = mesh.devices.shape
    side = math.isqrt(wide // 2)
    fine = Mesh(mesh.devices.reshape(side, side, 2, narrow), EVERY)
    rows = P(EVERY, None)
    return jax.shard_map(
        shards,
        mesh=fine,
        in_specs=(rows,) * 5,
        out_specs=(rows,) * 4,
        check_vma=False,
    )
```

```python
import functools
import math

import jax
import jax.numpy as jnp
from jax import lax
from jax.experimental import pallas as pl
from jax.experimental.pallas import tpu as pltpu
from jax.sharding import Mesh, PartitionSpec as P

HIGH = lax.Precision.HIGHEST
PLANE = ("x", "y")
LINE = ("core", "z")
EVERY = ("x", "y", "core", "z")
PARAMS = pltpu.CompilerParams(vmem_limit_bytes=40 * 1024 * 1024)
LIGHT = pl.CostEstimate(flops=1, bytes_accessed=1, transcendentals=0)


def exchange(value, axes):
    return lax.all_to_all(value, axes, 0, 0, tiled=True)


def spread(block, axes):
    count = lax.axis_size(axes)
    return exchange(jnp.broadcast_to(block[None], (count, *block.shape)), axes)


def other_core(value):
    return lax.ppermute(value, "core", [(0, 1), (1, 0)])


def gather_plane(block):
    return spread(block, PLANE).reshape(-1, block.shape[1])


def scatter_plane(whole):
    chip = whole.reshape(lax.axis_size(PLANE), -1, whole.shape[1])
    return jnp.sum(exchange(chip, PLANE), axis=0)


def in_hbm(*values):
    return [pltpu.with_memory_space_constraint(v, pltpu.HBM) for v in values]


def call(kernel, shapes, memories, scratch=(), light=False, written=False, **options):
    return pl.pallas_call(
        kernel,
        out_shape=shapes,
        in_specs=[pl.BlockSpec(memory_space=m) for m in memories],
        out_specs=jax.tree.map(
            lambda s: pl.BlockSpec(
                memory_space=pl.ANY if s.memory_space == pltpu.HBM and not written else pltpu.VMEM
            ),
            shapes,
        ),
        scratch_shapes=list(scratch),
        compiler_params=PARAMS,
        cost_estimate=LIGHT if light else None,
        **options,
    )


def state_kernel(gate_ref, up_ref, out_ref):
    half = gate_ref.shape[0] // 2
    size = out_ref.shape[0] // 2
    for which, ref in enumerate((gate_ref, up_ref)):
        message = jnp.concatenate([ref[:half, :], ref[half:, :]], axis=1)
        for z in range(size):
            out_ref[which * size + z] = message


def state_messages(gate, up):
    rows, rank = gate.shape
    shape = (2 * lax.axis_size("z"), rows // 2, 2 * rank)
    return call(state_kernel, pltpu.VMEM(shape, gate.dtype), [pltpu.VMEM] * 2)(
        *in_hbm(gate, up)
    )


def write_line(got_ref, line_ref):
    size, half = got_ref.shape[0] // 2, got_ref.shape[1]
    rank = got_ref.shape[2] // 2
    for z in range(size):
        for part in range(2):
            columns = slice(part * rank, (part + 1) * rank)
            start = (2 * z + part) * half
            line_ref[start : start + half, :] = jnp.concatenate(
                [got_ref[z, :, columns], got_ref[size + z, :, columns]], axis=1
            )


def sum_kernel(parts_ref, after_ref, out_ref, line_ref):
    del after_ref
    line_ref[...] = jnp.sum(parts_ref[...], axis=0)
    size, half = out_ref.shape[0] // 2, out_ref.shape[1]
    rank = out_ref.shape[2] // 2
    for which in range(2):
        columns = slice(which * rank, (which + 1) * rank)
        for z in range(size):
            start = 2 * z * half
            out_ref[which * size + z] = jnp.concatenate(
                [
                    line_ref[start : start + half, columns],
                    line_ref[start + half : start + 2 * half, columns],
                ],
                axis=1,
            )


def sum_messages(parts, after):
    _, rows, columns = parts.shape
    size = lax.axis_size("z")
    return call(
        sum_kernel,
        pltpu.VMEM((2 * size, rows // (2 * size), columns), parts.dtype),
        [pltpu.VMEM, pl.ANY],
        [pltpu.VMEM((rows, columns), parts.dtype)],
    )(parts, after)


def sorted_blocks(count, value_ref):
    block = value_ref.shape[1] // (2 * count)
    for half in range(2):
        for i in range(count):
            start = (2 * i + half) * block
            place = (half * count + i) * block
            yield value_ref[:, start : start + block], slice(place, place + block)


def write_halves(count, value_ref, low_out, high_out):
    half = low_out.shape[1]
    for value, to in sorted_blocks(count, value_ref):
        if to.stop <= half:
            low_out[:, to] = value.astype(jnp.float32)
        else:
            high_out[:, to.start - half : to.stop - half] = value.astype(jnp.float32)


def give_grad_kernel(count, gate_ref, up_ref, low_out, high_out, buffer, sem):
    core = lax.axis_index("core")
    for which, ref in ((0, up_ref), (1, gate_ref)):

        @pl.when(core == which)
        def _(ref=ref):
            copy = pltpu.make_async_copy(ref, buffer, sem)
            copy.start()
            copy.wait()

    write_halves(count, buffer, low_out, high_out)


def give_grad(gate, up):
    count = lax.axis_size(PLANE)
    tokens, columns = gate.shape
    return call(
        functools.partial(give_grad_kernel, count),
        [pltpu.VMEM((tokens, columns // 2), jnp.float32)] * 2,
        [pl.ANY] * 2,
        [pltpu.VMEM((tokens, columns), gate.dtype), pltpu.SemaphoreType.DMA],
        light=True,
    )(*in_hbm(gate, up))


def turn(value):
    return value.astype(jnp.float32).T.astype(jnp.bfloat16)


def own_stores(outs, scratch):
    tokens = scratch[0].shape[0]
    staged, sems = scratch[2:6], scratch[6]
    return [
        pltpu.make_async_copy(
            staged[i],
            outs[i].at[:, :tokens] if i % 2 else outs[i].at[:tokens, :],
            sems.at[2 + i],
        )
        for i in range(4)
    ]


def own_part(count, act_ref, grad_ref, outs, scratch):
    staged, sems = scratch[2:6], scratch[6]
    loads = [
        pltpu.make_async_copy(ref, scratch[i], sems.at[i])
        for i, ref in enumerate((act_ref, grad_ref))
    ]
    for load in loads:
        load.start()
    stores = own_stores(outs, scratch)
    for i in range(2):
        rows, turned = staged[2 * i : 2 * i + 2]
        loads[i].wait()
        for value, to in sorted_blocks(count, scratch[i]):
            rows[:, to] = value
        stores[2 * i].start()
        turned[...] = turn(rows[...])
        stores[2 * i + 1].start()


def keep_kernel(count, got_ref, act_ref, gate_ref, lines_out, *refs):
    outs, scratch, (line_ref, line_sem) = refs[:4], refs[4:-2], refs[-2:]
    write_line(got_ref, line_ref)
    copies = [
        pltpu.make_async_copy(line_ref, lines_out.at[i], line_sem.at[i]) for i in range(count)
    ]
    for copy in copies:
        copy.start()

    @pl.when(lax.axis_index("core") == 0)
    def _():
        own_part(count, act_ref, gate_ref, outs, scratch)
        for store in own_stores(outs, scratch):
            store.wait()

    for copy in copies:
        copy.wait()


def keep_late_kernel(count, act_ref, up_ref, *refs):
    outs, (low_out, high_out), scratch = refs[4:8], refs[8:10], refs[10:]
    late = lax.axis_index("core") == 1

    @pl.when(late)
    def _():
        own_part(count, act_ref, up_ref, outs, scratch)

    @pl.when(jnp.logical_not(late))
    def _():
        load = pltpu.make_async_copy(act_ref, scratch[0], scratch[6].at[0])
        load.start()
        load.wait()

    write_halves(count, scratch[0], low_out, high_out)

    @pl.when(late)
    def _():
        for store in own_stores(outs, scratch):
            store.wait()


def merge_kernel(*refs):
    takes, outs = refs[:4], refs[8:12]
    buffers, staged, (load_sems, store_sems) = refs[12:16], refs[16:20], refs[20:]
    loads = [
        pltpu.make_async_copy(take, buffer, load_sems.at[i])
        for i, (take, buffer) in enumerate(zip(takes, buffers))
    ]
    for load in loads:
        load.start()
    tokens = buffers[0].shape[0]
    stores = []
    for i in (1, 0):
        rows, turned = staged[2 * i : 2 * i + 2]
        half = buffers[2 * i].shape[1]
        for j in range(2):
            loads[2 * i + j].wait()
            to = slice(j * half, (j + 1) * half)
            value = buffers[2 * i + j][...]
            rows[:, to] = value.astype(jnp.bfloat16)
            turned[to, :] = value.T.astype(jnp.bfloat16)
        stores += [
            pltpu.make_async_copy(rows, outs[2 * i].at[tokens:, :], store_sems.at[2 * i]),
            pltpu.make_async_copy(
                turned, outs[2 * i + 1].at[:, tokens:], store_sems.at[2 * i + 1]
            ),
        ]
        for store in stores[-2:]:
            store.start()
    for store in stores:
        store.wait()


def chip_arrays(act, gate, up, got):
    count = lax.axis_size(PLANE)
    tokens = act.shape[0]
    kinds = [
        (shape, act.dtype)
        for v in (act, gate)
        for shape in ((tokens, v.shape[1]), (v.shape[1], tokens))
    ]
    scratch = [
        pltpu.VMEM(act.shape, act.dtype),
        pltpu.VMEM(gate.shape, gate.dtype),
        *[pltpu.VMEM(*kind) for kind in kinds],
        pltpu.SemaphoreType.DMA((6,)),
    ]
    wholes = [
        pltpu.HBM(tuple(2 * n if n == tokens else n for n in shape), kind)
        for shape, kind in kinds
    ]
    line = got.shape[0] * got.shape[1], got.shape[2]
    lines, *partly = call(
        functools.partial(keep_kernel, count),
        [pltpu.HBM((count, *line), got.dtype), *wholes],
        [pltpu.VMEM, pl.ANY, pl.ANY],
        [*scratch, pltpu.VMEM(line, got.dtype), pltpu.SemaphoreType.DMA((count,))],
        light=True,
    )(got, *in_hbm(act, gate))

    half = pltpu.VMEM((tokens, act.shape[1] // 2), jnp.float32)
    *partly, low, high = call(
        functools.partial(keep_late_kernel, count),
        [*wholes, half, half],
        [pl.ANY] * 6,
        scratch,
        light=True,
        input_output_aliases={2 + i: i for i in range(4)},
    )(*in_hbm(act, up), *partly)

    grads = [other_core(piece) for piece in give_grad(gate, up)]
    taken = [other_core(low), other_core(high), *grads]
    return lines, call(
        merge_kernel,
        wholes,
        [pl.ANY] * 8,
        [
            *[pltpu.VMEM(t.shape, t.dtype) for t in taken],
            *scratch[2:6],
            *[pltpu.SemaphoreType.DMA((4,))] * 2,
        ],
        light=True,
        input_output_aliases={4 + i: i for i in range(4)},
    )(*taken, *partly)


def halves(value):
    high = value.astype(jnp.bfloat16)
    low = (value - high.astype(jnp.float32)).astype(jnp.bfloat16)
    return jnp.concatenate([high, low], axis=1)


def fold(value):
    columns = value.shape[1] // 2
    return value[:, :columns] + value[:, columns:]


def product(left, right):
    return fold(jnp.dot(left, right, preferred_element_type=jnp.float32))


def joined(low, high):
    lane = lax.broadcasted_iota(jnp.int32, low.shape, 1)
    return jnp.where(lane < low.shape[1] // 2, low, high)


def doubled(value):
    return value + pltpu.roll(value, value.shape[1] // 2, 1)


def small_kernel(grad_ref, state_ref, out_ref, buffer, sems):
    steps = sems.shape[0]
    step = grad_ref.shape[0] // steps
    copies = []
    for i in range(steps):
        at = slice(i * step, (i + 1) * step)
        copies.append(pltpu.make_async_copy(grad_ref.at[at, :], buffer.at[at, :], sems.at[i]))
        copies[-1].start()
    state = halves(state_ref[...])
    columns = state.shape[0]
    for i in range(steps):
        at = slice(i * step, (i + 1) * step)
        copies[i].wait()
        out_ref[at, :] = doubled(
            joined(product(buffer[at, :columns], state), product(buffer[at, columns:], state))
        )


def tall_kernel(turned_ref, factor_ref, out_ref):
    factor = halves(factor_ref[...])
    rows = out_ref.shape[0]
    out_ref[...] = joined(
        product(turned_ref[:rows, :], factor), product(turned_ref[rows:, :], factor)
    )


def tall_product(turned, factor):
    shape = (turned.shape[0] // 2, factor.shape[1])
    return call(tall_kernel, pltpu.VMEM(shape, jnp.float32), [pltpu.VMEM] * 2)(turned, factor)


def streamed_kernel(turned_ref, factor_ref, out_ref, staged, sems):
    factor = halves(factor_ref[...])
    steps = sems.shape[0]
    rows = out_ref.shape[0]
    step = rows // steps
    copies = []
    for i in range(steps):
        at = slice(i * step, (i + 1) * step)
        other = slice(rows + i * step, rows + (i + 1) * step)
        staged[at, :] = joined(
            product(turned_ref[at, :], factor), product(turned_ref[other, :], factor)
        )
        copies.append(pltpu.make_async_copy(staged.at[at, :], out_ref.at[at, :], sems.at[i]))
        copies[-1].start()
    for copy in copies:
        copy.wait()


def streamed_product(turned, factor):
    shape = (turned.shape[0] // 2, factor.shape[1])
    return call(
        streamed_kernel,
        pltpu.HBM(shape, jnp.float32),
        [pltpu.VMEM] * 2,
        [pltpu.VMEM(shape, jnp.float32), pltpu.SemaphoreType.DMA((4,))],
    )(turned, factor)


def project_kernel(factor, rows_ref, raw_ref, out_ref):
    raw = halves(raw_ref[...])
    columns = raw.shape[0]
    out_ref[...] = factor * doubled(
        joined(product(rows_ref[:, :columns], raw), product(rows_ref[:, columns:], raw))
    )


def pack_kernel(after_ref, inverse_ref, rows_ref, out_ref):
    del after_ref
    rank = inverse_ref.shape[0]
    out_ref[:rank, :rank] = inverse_ref[...]
    out_ref[:rank, rank:] = jnp.zeros_like(inverse_ref)
    out_ref[rank:, :] = rows_ref[...]


def pack(after, inverse, rows):
    shape = (inverse.shape[0] + rows.shape[0], rows.shape[1])
    return call(
        pack_kernel, pltpu.VMEM(shape, jnp.float32), [pl.ANY, pltpu.VMEM, pltpu.VMEM], light=True
    )(after, inverse, rows)


def end_kernel(stretch, parts_ref, mine_ref, other_ref, *outs):
    rank = outs[0].shape[1]
    core = lax.axis_index("core")

    def dot(left, right):
        return jnp.dot(left, right, precision=HIGH, preferred_element_type=jnp.float32)

    def write(own):
        for which, ref in enumerate((mine_ref, other_ref) if own == 0 else (other_ref, mine_ref)):
            inverse = ref[:rank, :rank]
            rows = ref[rank:, own * rank : (own + 1) * rank]
            outs[2 * which][...] = dot(rows, inverse) * stretch
            size = parts_ref.shape[0] // 2
            message = jnp.sum(parts_ref[which * size : (which + 1) * size], axis=0)
            summed = jnp.concatenate([message[:, :rank], message[:, rank:]], axis=0)
            outs[2 * which + 1][...] = dot(summed, inverse)

    pl.when(core == 0)(lambda: write(0))
    pl.when(core == 1)(lambda: write(1))


def shards(activations, grad_gate, grad_up, state_gate, state_up):
    devices = lax.axis_size(EVERY)
    tokens, width = activations.shape
    factor = 1.0 / math.sqrt(tokens * devices)
    rows, rank = state_gate.shape
    both = 2 * rank
    line_size = lax.axis_size("z")

    got = exchange(state_messages(state_gate, state_up), LINE)
    lines, (act, act_turned, grad, grad_turned) = chip_arrays(
        activations, grad_gate, grad_up, got
    )
    state = exchange(lines, PLANE).reshape(-1, both)

    small = call(
        small_kernel,
        pltpu.VMEM((2 * tokens, both), jnp.float32),
        [pl.ANY, pltpu.VMEM],
        [pltpu.VMEM(grad.shape, grad.dtype), pltpu.SemaphoreType.DMA((2,))],
    )(*in_hbm(grad), state)
    summed = scatter_plane(tall_product(act_turned, small)).reshape(line_size, -1, both)
    mine = jnp.sum(exchange(summed, "z"), axis=0) * jnp.float32(factor)
    raw = gather_plane(spread(mine, "z").reshape(-1, both))

    project = call(
        functools.partial(project_kernel, factor),
        pltpu.VMEM((2 * tokens, both), jnp.float32),
        [pltpu.VMEM] * 2,
    )(act, raw)
    gram = lax.dot_general(
        raw, raw, (((0,), (0,)), ((), ())), precision=HIGH, preferred_element_type=jnp.float32
    )
    gram = gram[:rank, :rank] + gram[rank:, rank:]
    lower = jnp.linalg.cholesky(gram, symmetrize_input=False)
    inverse = lax.linalg.triangular_solve(
        lower, jnp.eye(rank, dtype=jnp.float32), left_side=False, lower=True, transpose_a=True
    )

    partial = streamed_product(grad_turned, project)
    received = exchange(partial.reshape(lax.axis_size(PLANE), -1, both), PLANE)
    messages = sum_messages(received, inverse)
    parts = exchange(messages, LINE)
    packed = pack(messages, inverse, mine)

    shapes = [pltpu.HBM((n, rank), jnp.float32) for _ in range(2) for n in (mine.shape[0], rows)]
    return tuple(
        call(
            functools.partial(end_kernel, math.sqrt(width)), shapes, [pltpu.VMEM] * 3, written=True
        )(parts, packed, other_core(packed))
    )


def solution(mesh):
    wide, narrow = mesh.devices.shape
    side = math.isqrt(wide // 2)
    fine = Mesh(mesh.devices.reshape(side, side, 2, narrow), EVERY)
    rows = P(EVERY, None)
    return jax.shard_map(
        shards,
        mesh=fine,
        in_specs=(rows,) * 5,
        out_specs=(rows,) * 4,
        check_vma=False,
    )
```

```python
import functools
import math

import jax
import jax.numpy as jnp
from jax import lax
from jax.experimental import pallas as pl
from jax.experimental.pallas import tpu as pltpu
from jax.sharding import Mesh, PartitionSpec as P

HIGH = lax.Precision.HIGHEST
PLANE = ("x", "y")
LINE = ("core", "z")
EVERY = ("x", "y", "core", "z")
SPARE = 8
PARAMS = pltpu.CompilerParams(vmem_limit_bytes=40 * 1024 * 1024)
LIGHT = pl.CostEstimate(flops=1, bytes_accessed=1, transcendentals=0)


def exchange(value, axes):
    return lax.all_to_all(value, axes, 0, 0, tiled=True)


def spread(block, axes):
    count = lax.axis_size(axes)
    return exchange(jnp.broadcast_to(block[None], (count, *block.shape)), axes)


def other_core(value):
    return lax.ppermute(value, "core", [(0, 1), (1, 0)])


def gather_plane(block):
    return spread(block, PLANE).reshape(-1, block.shape[1])


def scatter_plane(whole):
    chip = whole.reshape(lax.axis_size(PLANE), -1, whole.shape[1])
    return jnp.sum(exchange(chip, PLANE), axis=0)


def in_hbm(*values):
    return [pltpu.with_memory_space_constraint(v, pltpu.HBM) for v in values]


def call(kernel, shapes, memories, scratch=(), light=False, written=False, **options):
    return pl.pallas_call(
        kernel,
        out_shape=shapes,
        in_specs=[pl.BlockSpec(memory_space=m) for m in memories],
        out_specs=jax.tree.map(
            lambda s: pl.BlockSpec(
                memory_space=pl.ANY if s.memory_space == pltpu.HBM and not written else pltpu.VMEM
            ),
            shapes,
        ),
        scratch_shapes=list(scratch),
        compiler_params=PARAMS,
        cost_estimate=LIGHT if light else None,
        **options,
    )


def state_kernel(gate_ref, up_ref, out_ref):
    half = gate_ref.shape[0] // 2
    size = out_ref.shape[0] // 2
    for which, ref in enumerate((gate_ref, up_ref)):
        value = ref[...]
        message = jnp.concatenate([value[:half, :], value[half:, :]], axis=1)
        for z in range(size):
            out_ref[which * size + z] = message


def state_messages(gate, up):
    rows, rank = gate.shape
    shape = (2 * lax.axis_size("z"), rows // 2, 2 * rank)
    return call(state_kernel, pltpu.VMEM(shape, gate.dtype), [pltpu.VMEM] * 2)(
        *in_hbm(gate, up)
    )


def write_line(got_ref, line_ref):
    size, half = got_ref.shape[0] // 2, got_ref.shape[1]
    rank = got_ref.shape[2] // 2
    for z in range(size):
        for part in range(2):
            columns = slice(part * rank, (part + 1) * rank)
            start = (2 * z + part) * half
            line_ref[start : start + half, :] = jnp.concatenate(
                [got_ref[z, :, columns], got_ref[size + z, :, columns]], axis=1
            )


def sum_kernel(parts_ref, after_ref, out_ref, line_ref):
    del after_ref
    line_ref[: parts_ref.shape[1], :] = jnp.sum(parts_ref[...], axis=0)
    size, half = out_ref.shape[0] // 2, out_ref.shape[1]
    rank = out_ref.shape[2] // 2
    for which in range(2):
        columns = slice(which * rank, (which + 1) * rank)
        for z in range(size):
            start = 2 * z * half
            out_ref[which * size + z] = jnp.concatenate(
                [
                    line_ref[start : start + half, columns],
                    line_ref[start + half : start + 2 * half, columns],
                ],
                axis=1,
            )


def sum_messages(parts, after):
    _, rows, columns = parts.shape
    size = lax.axis_size("z")
    return call(
        sum_kernel,
        pltpu.VMEM((2 * size, rows // (2 * size), columns), parts.dtype),
        [pltpu.VMEM, pl.ANY],
        [pltpu.VMEM((rows + SPARE, columns), parts.dtype)],
    )(parts, after)


def sorted_blocks(count, value_ref):
    block = value_ref.shape[1] // (2 * count)
    for half in range(2):
        for i in range(count):
            start = (2 * i + half) * block
            place = (half * count + i) * block
            yield value_ref[:, start : start + block], slice(place, place + block)


def write_halves(count, value_ref, low_out, high_out):
    half = low_out.shape[1]
    for value, to in sorted_blocks(count, value_ref):
        if to.stop <= half:
            low_out[:, to] = value.astype(jnp.float32)
        else:
            high_out[:, to.start - half : to.stop - half] = value.astype(jnp.float32)


def give_grad_kernel(count, gate_ref, up_ref, low_out, high_out, buffer, sem):
    core = lax.axis_index("core")
    for which, ref in ((0, up_ref), (1, gate_ref)):

        @pl.when(core == which)
        def _(ref=ref):
            copy = pltpu.make_async_copy(ref, buffer, sem)
            copy.start()
            copy.wait()

    write_halves(count, buffer, low_out, high_out)


def give_grad(gate, up):
    count = lax.axis_size(PLANE)
    tokens, columns = gate.shape
    return call(
        functools.partial(give_grad_kernel, count),
        [pltpu.VMEM((tokens, columns // 2), jnp.float32)] * 2,
        [pl.ANY] * 2,
        [pltpu.VMEM((tokens, columns), gate.dtype), pltpu.SemaphoreType.DMA],
        light=True,
    )(*in_hbm(gate, up))


def turn(value):
    return value.astype(jnp.float32).T.astype(jnp.bfloat16)


def own_stores(outs, scratch):
    tokens = scratch[0].shape[0]
    staged, sems = scratch[2:6], scratch[6]
    return [
        pltpu.make_async_copy(
            staged[i],
            outs[i].at[:, :tokens] if i % 2 else outs[i].at[:tokens, :],
            sems.at[2 + i],
        )
        for i in range(4)
    ]


def own_part(count, act_ref, grad_ref, outs, scratch):
    staged, sems = scratch[2:6], scratch[6]
    loads = [
        pltpu.make_async_copy(ref, scratch[i], sems.at[i])
        for i, ref in enumerate((act_ref, grad_ref))
    ]
    for load in loads:
        load.start()
    stores = own_stores(outs, scratch)
    for i in range(2):
        rows, turned = staged[2 * i : 2 * i + 2]
        loads[i].wait()
        for value, to in sorted_blocks(count, scratch[i]):
            rows[:, to] = value
        stores[2 * i].start()
        turned[...] = turn(rows[...])
        stores[2 * i + 1].start()


def keep_kernel(count, got_ref, act_ref, gate_ref, lines_out, *refs):
    outs, scratch, (line_ref, line_sem) = refs[:4], refs[4:-2], refs[-2:]
    write_line(got_ref, line_ref)
    rows = pl.ds(0, lines_out.shape[1])
    copies = [
        pltpu.make_async_copy(line_ref.at[rows, :], lines_out.at[i], line_sem.at[i])
        for i in range(count)
    ]
    for copy in copies:
        copy.start()

    @pl.when(lax.axis_index("core") == 0)
    def _():
        own_part(count, act_ref, gate_ref, outs, scratch)
        for store in own_stores(outs, scratch):
            store.wait()

    for copy in copies:
        copy.wait()


def keep_late_kernel(count, act_ref, up_ref, *refs):
    outs, (low_out, high_out), scratch = refs[4:8], refs[8:10], refs[10:]
    late = lax.axis_index("core") == 1

    @pl.when(late)
    def _():
        own_part(count, act_ref, up_ref, outs, scratch)

    @pl.when(jnp.logical_not(late))
    def _():
        load = pltpu.make_async_copy(act_ref, scratch[0], scratch[6].at[0])
        load.start()
        load.wait()

    write_halves(count, scratch[0], low_out, high_out)

    @pl.when(late)
    def _():
        for store in own_stores(outs, scratch):
            store.wait()


def merge_kernel(*refs):
    takes, outs = refs[:4], refs[8:12]
    buffers, staged, (load_sems, store_sems) = refs[12:16], refs[16:20], refs[20:]
    loads = [
        pltpu.make_async_copy(take, buffer, load_sems.at[i])
        for i, (take, buffer) in enumerate(zip(takes, buffers))
    ]
    for load in loads:
        load.start()
    tokens = buffers[0].shape[0]
    stores = []
    for i in (1, 0):
        rows, turned = staged[2 * i : 2 * i + 2]
        half = buffers[2 * i].shape[1]
        for j in range(2):
            loads[2 * i + j].wait()
            to = slice(j * half, (j + 1) * half)
            value = buffers[2 * i + j][...]
            rows[:, to] = value.astype(jnp.bfloat16)
            turned[to, :] = value.T.astype(jnp.bfloat16)
        stores += [
            pltpu.make_async_copy(rows, outs[2 * i].at[tokens:, :], store_sems.at[2 * i]),
            pltpu.make_async_copy(
                turned, outs[2 * i + 1].at[:, tokens:], store_sems.at[2 * i + 1]
            ),
        ]
        for store in stores[-2:]:
            store.start()
    for store in stores:
        store.wait()


def chip_arrays(act, gate, up, got):
    count = lax.axis_size(PLANE)
    tokens = act.shape[0]
    kinds = [
        (shape, act.dtype)
        for v in (act, gate)
        for shape in ((tokens, v.shape[1]), (v.shape[1], tokens))
    ]
    scratch = [
        pltpu.VMEM(act.shape, act.dtype),
        pltpu.VMEM(gate.shape, gate.dtype),
        *[pltpu.VMEM(*kind) for kind in kinds],
        pltpu.SemaphoreType.DMA((6,)),
    ]
    wholes = [
        pltpu.HBM(tuple(2 * n if n == tokens else n for n in shape), kind)
        for shape, kind in kinds
    ]
    line = got.shape[0] * got.shape[1], got.shape[2]
    lines, *partly = call(
        functools.partial(keep_kernel, count),
        [pltpu.HBM((count, *line), got.dtype), *wholes],
        [pltpu.VMEM, pl.ANY, pl.ANY],
        [*scratch, pltpu.VMEM((line[0] + SPARE, line[1]), got.dtype), pltpu.SemaphoreType.DMA((count,))],
        light=True,
    )(got, *in_hbm(act, gate))

    half = pltpu.VMEM((tokens, act.shape[1] // 2), jnp.float32)
    *partly, low, high = call(
        functools.partial(keep_late_kernel, count),
        [*wholes, half, half],
        [pl.ANY] * 6,
        scratch,
        light=True,
        input_output_aliases={2 + i: i for i in range(4)},
    )(*in_hbm(act, up), *partly)

    grads = [other_core(piece) for piece in give_grad(gate, up)]
    taken = [other_core(low), other_core(high), *grads]
    return lines, call(
        merge_kernel,
        wholes,
        [pl.ANY] * 8,
        [
            *[pltpu.VMEM(t.shape, t.dtype) for t in taken],
            *scratch[2:6],
            *[pltpu.SemaphoreType.DMA((4,))] * 2,
        ],
        light=True,
        input_output_aliases={4 + i: i for i in range(4)},
    )(*taken, *partly)


def halves(value):
    high = value.astype(jnp.bfloat16)
    low = (value - high.astype(jnp.float32)).astype(jnp.bfloat16)
    return jnp.concatenate([high, low], axis=1)


def fold(value):
    columns = value.shape[1] // 2
    return value[:, :columns] + value[:, columns:]


def product(left, right):
    return fold(jnp.dot(left, right, preferred_element_type=jnp.float32))


def joined(low, high):
    lane = lax.broadcasted_iota(jnp.int32, low.shape, 1)
    return jnp.where(lane < low.shape[1] // 2, low, high)


def doubled(value):
    return value + pltpu.roll(value, value.shape[1] // 2, 1)


def small_kernel(grad_ref, state_ref, out_ref, buffer, sems):
    steps = sems.shape[0]
    step = grad_ref.shape[0] // steps
    copies = []
    for i in range(steps):
        at = slice(i * step, (i + 1) * step)
        copies.append(pltpu.make_async_copy(grad_ref.at[at, :], buffer.at[at, :], sems.at[i]))
        copies[-1].start()
    state = halves(state_ref[...])
    columns = state.shape[0]
    for i in range(steps):
        at = slice(i * step, (i + 1) * step)
        copies[i].wait()
        out_ref[at, :] = doubled(
            joined(product(buffer[at, :columns], state), product(buffer[at, columns:], state))
        )


def tall_kernel(turned_ref, factor_ref, out_ref):
    factor = halves(factor_ref[...])
    rows = out_ref.shape[0]
    out_ref[...] = joined(
        product(turned_ref[:rows, :], factor), product(turned_ref[rows:, :], factor)
    )


def tall_product(turned, factor):
    shape = (turned.shape[0] // 2, factor.shape[1])
    return call(tall_kernel, pltpu.VMEM(shape, jnp.float32), [pltpu.VMEM] * 2)(turned, factor)


def streamed_kernel(turned_ref, factor_ref, out_ref, staged, sems):
    factor = halves(factor_ref[...])
    steps = sems.shape[0]
    rows = out_ref.shape[0]
    step = rows // steps
    copies = []
    for i in range(steps):
        at = slice(i * step, (i + 1) * step)
        other = slice(rows + i * step, rows + (i + 1) * step)
        staged[at, :] = joined(
            product(turned_ref[at, :], factor), product(turned_ref[other, :], factor)
        )
        copies.append(pltpu.make_async_copy(staged.at[at, :], out_ref.at[at, :], sems.at[i]))
        copies[-1].start()
    for copy in copies:
        copy.wait()


def streamed_product(turned, factor):
    shape = (turned.shape[0] // 2, factor.shape[1])
    return call(
        streamed_kernel,
        pltpu.HBM(shape, jnp.float32),
        [pltpu.VMEM] * 2,
        [pltpu.VMEM(shape, jnp.float32), pltpu.SemaphoreType.DMA((4,))],
    )(turned, factor)


def project_kernel(factor, rows_ref, raw_ref, out_ref):
    raw = halves(raw_ref[...])
    columns = raw.shape[0]
    out_ref[...] = factor * doubled(
        joined(product(rows_ref[:, :columns], raw), product(rows_ref[:, columns:], raw))
    )


def pack_kernel(after_ref, inverse_ref, rows_ref, out_ref):
    del after_ref
    rank = inverse_ref.shape[0]
    out_ref[:rank, :rank] = inverse_ref[...]
    out_ref[:rank, rank:] = jnp.zeros_like(inverse_ref)
    out_ref[rank:, :] = rows_ref[...]


def pack(after, inverse, rows):
    shape = (inverse.shape[0] + rows.shape[0], rows.shape[1])
    return call(
        pack_kernel, pltpu.VMEM(shape, jnp.float32), [pl.ANY, pltpu.VMEM, pltpu.VMEM], light=True
    )(after, inverse, rows)


def end_kernel(stretch, parts_ref, mine_ref, other_ref, *outs):
    rank = outs[0].shape[1]
    core = lax.axis_index("core")

    def dot(left, right):
        return jnp.dot(left, right, precision=HIGH, preferred_element_type=jnp.float32)

    def write(own):
        for which, ref in enumerate((mine_ref, other_ref) if own == 0 else (other_ref, mine_ref)):
            inverse = ref[:rank, :rank]
            rows = ref[rank:, own * rank : (own + 1) * rank]
            outs[2 * which][...] = dot(rows, inverse) * stretch
            size = parts_ref.shape[0] // 2
            message = jnp.sum(parts_ref[which * size : (which + 1) * size], axis=0)
            summed = jnp.concatenate([message[:, :rank], message[:, rank:]], axis=0)
            outs[2 * which + 1][...] = dot(summed, inverse)

    pl.when(core == 0)(lambda: write(0))
    pl.when(core == 1)(lambda: write(1))


def shards(activations, grad_gate, grad_up, state_gate, state_up):
    devices = lax.axis_size(EVERY)
    tokens, width = activations.shape
    factor = 1.0 / math.sqrt(tokens * devices)
    rows, rank = state_gate.shape
    both = 2 * rank
    line_size = lax.axis_size("z")

    got = exchange(state_messages(state_gate, state_up), LINE)
    lines, (act, act_turned, grad, grad_turned) = chip_arrays(
        activations, grad_gate, grad_up, got
    )
    state = exchange(lines, PLANE).reshape(-1, both)

    small = call(
        small_kernel,
        pltpu.VMEM((2 * tokens, both), jnp.float32),
        [pl.ANY, pltpu.VMEM],
        [pltpu.VMEM(grad.shape, grad.dtype), pltpu.SemaphoreType.DMA((2,))],
    )(*in_hbm(grad), state)
    summed = scatter_plane(tall_product(act_turned, small)).reshape(line_size, -1, both)
    mine = jnp.sum(exchange(summed, "z"), axis=0) * jnp.float32(factor)
    raw = gather_plane(spread(mine, "z").reshape(-1, both))

    project = call(
        functools.partial(project_kernel, factor),
        pltpu.VMEM((2 * tokens, both), jnp.float32),
        [pltpu.VMEM] * 2,
    )(act, raw)
    gram = lax.dot_general(
        raw, raw, (((0,), (0,)), ((), ())), precision=HIGH, preferred_element_type=jnp.float32
    )
    gram = gram[:rank, :rank] + gram[rank:, rank:]
    lower = jnp.linalg.cholesky(gram, symmetrize_input=False)
    inverse = lax.linalg.triangular_solve(
        lower, jnp.eye(rank, dtype=jnp.float32), left_side=False, lower=True, transpose_a=True
    )

    partial = streamed_product(grad_turned, project)
    received = exchange(partial.reshape(lax.axis_size(PLANE), -1, both), PLANE)
    messages = sum_messages(received, inverse)
    parts = exchange(messages, LINE)
    packed = pack(messages, inverse, mine)

    shapes = [pltpu.HBM((n, rank), jnp.float32) for _ in range(2) for n in (mine.shape[0], rows)]
    return tuple(
        call(
            functools.partial(end_kernel, math.sqrt(width)), shapes, [pltpu.VMEM] * 3, written=True
        )(parts, packed, other_core(packed))
    )


def solution(mesh):
    wide, narrow = mesh.devices.shape
    side = math.isqrt(wide // 2)
    fine = Mesh(mesh.devices.reshape(side, side, 2, narrow), EVERY)
    rows = P(EVERY, None)
    return jax.shard_map(
        shards,
        mesh=fine,
        in_specs=(rows,) * 5,
        out_specs=(rows,) * 4,
        check_vma=False,
    )
```
